32 devices in a mesh: rows: 16 (over z, y, core), cols: 2 (over x).
Axes of the slice: x: 2, y: 2, z: 4, core: 2. Of those that a mesh axis runs over, the one named last changes fastest.
Arguments:
- start: float32 [16, 32768], P('cols', 'rows'), may hold values from -18 to 18
- weights: bfloat16 [256, 8, 128, 128], P('rows'), may hold values from 0 to 2, as said below
- block_count: int32 [256], P('rows'), may hold values from 1 to 8
- col_ids: int32 [256, 8], P('rows'), may hold values from 0 to 23
- send_ids: int32 [64, 2], P('rows'), may hold values from 0 to 15
- mixing: float32 [2, 16, 16], replicated, may hold values from -0.3 to 1.3
Outputs:
- subspace: float32 [16, 32768], P('cols', 'rows')
The draws below stay inside these ranges and needn't reach their ends.
Inputs may be any that keep to these rules, and one draw needn't show every extreme that they name: `weights`: about one entry in 32 is nonzero, all nonzero entries positive.
All inputs are finite; a program needn't handle non-finite values.
Results may differ from the reference program's by a relative error of at most 0.034.
Values may be sent and summed in bfloat16 or wider, within the bound.
A program may use at most 64 MiB of HBM per device.

```python
import jax
import jax.numpy as jnp
from jax import lax

K = 16
TILE = 128
NB = 8
REACH = 2
SLOTS = 2
DEGREE = 4
ITERS = 2
TILES_DEV = 16
TILES = 256
NPTS = 32768
NBUF = 24
N_ROWS = 16


def draw_start(key, part):
    first = jax.random.fold_in(key, 0)
    position = jnp.arange(NPTS, dtype=jnp.float32)[None, :] / (NPTS - 1)
    values = jnp.clip(jax.random.normal(first, (K, NPTS), jnp.float32), -6.0, 6.0)
    return values * (1.0 + 2.0 * position)


def draw_weights(key, part):
    first, second = jax.random.split(key)
    shape = (TILES, NB, TILE, TILE)
    present = (jax.random.randint(first, shape, 0, 32) == 0).astype(jnp.float32)
    values = jax.random.uniform(second, shape, jnp.float32, 0.2, 1.0)
    return (present * values).astype(jnp.bfloat16)


def draw_mixing(key, part):
    noise = 0.075 * jnp.clip(jax.random.normal(key, (ITERS, K, K), jnp.float32), -4.0, 4.0)
    return jnp.eye(K, dtype=jnp.float32)[None, :, :] + noise


def with_ends(drawn, own_key, smallest, high):
    extent = drawn.shape
    index_at = [jax.random.randint(jax.random.fold_in(own_key, axis), (), 0, extent[axis]) for axis in range(len(extent))]
    drawn = drawn.at[tuple(index_at)].set(smallest)
    longest = extent.index(max(extent))
    index_at[longest] = (index_at[longest] + 1) % extent[longest]
    return drawn.at[tuple(index_at)].set(high)


def setup_inputs(seed: int = 0) -> dict:
    seeds = jax.random.split(jax.random.key(seed), 7)
    start = draw_start(jax.random.fold_in(seeds[6], 71), 0)
    weights = draw_weights(jax.random.fold_in(seeds[6], 71), 0)
    block_count = with_ends(jax.random.randint(seeds[2], (TILES,), 1, NB + 1), jax.random.fold_in(seeds[2], 1), 1, NB).astype(jnp.int32)
    col_ids = with_ends(jax.random.randint(seeds[3], (TILES, NB), 0, NBUF), jax.random.fold_in(seeds[3], 1), 0, NBUF - 1).astype(jnp.int32)
    send_ids = with_ends(jax.random.randint(seeds[4], (N_ROWS * 2 * REACH, SLOTS), 0, TILES_DEV), jax.random.fold_in(seeds[4], 1), 0, TILES_DEV - 1).astype(jnp.int32)
    mixing = draw_mixing(jax.random.fold_in(seeds[6], 71), 0)
    return {"start": start, "weights": weights, "block_count": block_count, "col_ids": col_ids, "send_ids": send_ids, "mixing": mixing}


filter_center = 1.2
filter_half = 0.8

def source_tiles(col_ids, send_ids):
    owner = (jnp.arange(TILES, dtype=jnp.int32) // TILES_DEV)[:, None]
    local = col_ids < TILES_DEV
    slot_index = jnp.maximum(col_ids - TILES_DEV, 0)
    offset = slot_index // SLOTS
    within = slot_index % SLOTS
    distance = jnp.where(offset < REACH, offset - REACH, offset - REACH + 1)
    sender = owner - distance
    valid = (sender >= 0) & (sender < N_ROWS)
    sender_safe = jnp.clip(sender, 0, N_ROWS - 1)
    sent_tile = send_ids[sender_safe * (2 * REACH) + offset, within]
    remote = jnp.where(valid, sender_safe * TILES_DEV + sent_tile, TILES)
    return jnp.where(local, owner * TILES_DEV + col_ids, remote).astype(jnp.int32)

def group_degree(group):
    return lax.optimization_barrier(jnp.sum(group, axis=(1, 3), dtype=jnp.float32))

def apply_laplacian(vectors, scale, grouped, sources):
    scaled = (scale * vectors).astype(jnp.bfloat16)
    padded = jnp.concatenate([scaled, jnp.zeros((1, K, TILE), jnp.bfloat16)], 0)

    def one_group(pair):
        block_weights, block_sources = pair
        picked = padded[block_sources].astype(jnp.float32)
        return jnp.einsum('tbic,tbkc->tki', block_weights.astype(jnp.float32), picked)
    products = lax.map(one_group, (grouped, sources)).reshape(TILES, K, TILE)
    return vectors - scale * (products + scaled.astype(jnp.float32))

def reference(start, weights, block_count, col_ids, send_ids, mixing):
    live = jnp.arange(NB, dtype=jnp.int32)[None, :] < block_count[:, None]
    weights_live = jnp.where(live[:, :, None, None], weights, jnp.zeros((), jnp.bfloat16))
    grouped = weights_live.reshape(N_ROWS, TILES_DEV, NB, TILE, TILE)
    sources = source_tiles(col_ids, send_ids).reshape(N_ROWS, TILES_DEV, NB)
    degree = 1.0 + lax.map(group_degree, grouped).reshape(TILES, TILE)
    scale = lax.rsqrt(degree)[:, None, :]
    vectors = start.reshape(K, TILES, TILE).transpose(1, 0, 2)
    for iteration in range(ITERS):
        previous = vectors
        current = (apply_laplacian(previous, scale, grouped, sources) - filter_center * previous) / filter_half
        for order in range(DEGREE - 1):
            following = 2.0 * (apply_laplacian(current, scale, grouped, sources) - filter_center * current) / filter_half - previous
            previous, current = (current, following)
        flat = current.transpose(1, 0, 2).reshape(K, NPTS)
        gram = jnp.dot(flat, flat.T, precision=lax.Precision.HIGHEST) / NPTS
        lower = jnp.linalg.cholesky(gram)
        inverse = lax.linalg.triangular_solve(lower, jnp.eye(K, dtype=jnp.float32), left_side=True, lower=True)
        combined = jnp.dot(mixing[iteration], inverse, precision=lax.Precision.HIGHEST)
        vectors = jnp.einsum('kl,tli->tki', combined, current, precision=lax.Precision.HIGHEST)
    return vectors.transpose(1, 0, 2).reshape(K, NPTS)
```

```python
import functools

import jax
import jax.numpy as jnp
from jax import lax
from jax.experimental import pallas as pl
from jax.experimental.pallas import tpu as pltpu
from jax.sharding import PartitionSpec as P

K = 16
NB = 8
REACH = 2
SLOTS = 2
DEGREE = 4
ITERS = 2
SUB = 8
TILE = 128

filter_center = 1.2
filter_half = 0.8

MESH = pl.DeviceIdType.MESH
DISTANCES = [p - REACH if p < REACH else p - REACH + 1 for p in range(2 * REACH)]


def kernel(
    n, nx, group, col_width, tiles, total_points,
    block_count, col_ids, send_ids, start_ref, mixing_ref, weights_hbm,
    out_ref,
    w_ref, scale_ref, prev_ref, cur_ref, buf, outgoing, incoming, columns, gram_a, gram_b,
    w_sem, send_sem, recv_sem, col_send, col_recv, a_send, a_recv, b_send, b_recv,
):
    r = lax.axis_index("rows")
    x = lax.axis_index("cols")
    n_groups = n // group
    my_group, my_place = r // group, r % group

    barrier = pltpu.get_barrier_semaphore()
    greeted = (nx - 1) + (group - 1) + (n_groups - 1)
    for d in DISTANCES:
        reach = jnp.logical_and(r + d >= 0, r + d < n)

        @pl.when(reach)
        def _():
            pl.semaphore_signal(barrier, inc=1, device_id=(r + d, x), device_id_type=MESH)

        greeted = greeted + reach.astype(jnp.int32)
    for j in range(1, nx):
        pl.semaphore_signal(barrier, inc=1, device_id=(r, (x + j) % nx), device_id_type=MESH)
    for j in range(1, group):
        pl.semaphore_signal(
            barrier, inc=1, device_id=(my_group * group + (my_place + j) % group, x), device_id_type=MESH
        )
    for j in range(1, n_groups):
        pl.semaphore_signal(
            barrier, inc=1, device_id=((my_group + j) % n_groups * group + my_place, x), device_id_type=MESH
        )

    loads = [pltpu.make_async_copy(weights_hbm.at[t], w_ref.at[t], w_sem.at[t]) for t in range(tiles)]
    for load in loads:
        load.start()

    def times_tile(t, blocks):
        w = jnp.concatenate([w_ref[t, b] for b in range(NB)], 1)
        return lax.dot_general(
            blocks, w, (((1,), (1,)), ((), ())), preferred_element_type=jnp.float32
        )

    zeros = jnp.zeros((SUB, TILE), jnp.float32)
    for slot in range(tiles, tiles + 2 * REACH * SLOTS + 1):
        buf[slot] = zeros
    prev_ref[...] = start_ref[...]
    cur_ref[...] = start_ref[...]
    gram_a[...] = jnp.zeros_like(gram_a)
    for t in range(tiles):
        loads[t].wait()
        ones = [
            jnp.full((SUB, TILE), jnp.where(b < block_count[t], 1.0, 0.0), jnp.float32) for b in range(NB)
        ]
        degree = 1.0 + times_tile(t, jnp.concatenate(ones, 1).astype(jnp.bfloat16))
        scale_ref[:, t * TILE : (t + 1) * TILE] = lax.rsqrt(degree)

    pl.semaphore_wait(barrier, greeted)

    def neighbour_copy(step, o):
        return pltpu.make_async_remote_copy(
            src_ref=outgoing.at[step, o],
            dst_ref=incoming.at[step, o],
            send_sem=send_sem.at[step, o],
            recv_sem=recv_sem.at[step, o],
            device_id=(r + DISTANCES[o], x),
            device_id_type=MESH,
        )

    def apply(iteration, order):
        step = iteration * DEGREE + order
        for t in range(tiles):
            at = slice(t * TILE, (t + 1) * TILE)
            scaled = (scale_ref[:, at] * cur_ref[:, at]).astype(jnp.bfloat16)
            buf[t] = scaled.astype(jnp.float32)
        for o, d in enumerate(DISTANCES):
            picked = jnp.concatenate([buf[send_ids[o, s]] for s in range(SLOTS)], 0)
            outgoing[step, o] = picked.astype(jnp.bfloat16)

            @pl.when(jnp.logical_and(r + d >= 0, r + d < n))
            def _():
                neighbour_copy(step, o).start()

        for o, d in enumerate(DISTANCES):

            @pl.when(jnp.logical_and(r - d >= 0, r - d < n))
            def _():
                neighbour_copy(step, o).wait_recv()
                arrived = incoming[step, o].astype(jnp.float32)
                for s in range(SLOTS):
                    buf[tiles + o * SLOTS + s] = arrived[s * SUB : (s + 1) * SUB]

        first = order == 0
        gain = jnp.where(first, 1.0 / filter_half, 2.0 / filter_half)
        keep = jnp.where(first, 0.0, 1.0)
        empty = tiles + 2 * REACH * SLOTS
        for t in range(tiles):
            at = slice(t * TILE, (t + 1) * TILE)
            count = block_count[t]
            blocks = [buf[jnp.where(b < count, col_ids[t, b], empty)] for b in range(NB)]
            product = times_tile(t, jnp.concatenate(blocks, 1).astype(jnp.bfloat16))
            current = cur_ref[:, at]
            laplacian = current - scale_ref[:, at] * (product + buf[t])
            following = gain * (laplacian - filter_center * current) - keep * prev_ref[:, at]
            prev_ref[:, at] = current
            cur_ref[:, at] = following
        for o, d in enumerate(DISTANCES):

            @pl.when(jnp.logical_and(r + d >= 0, r + d < n))
            def _():
                neighbour_copy(step, o).wait_send()

    def exchange(copies):
        for copy in copies:
            copy.start()
        for copy in copies:
            copy.wait_recv()
        return copies

    def orthonormalize(iteration):
        columns[iteration, x] = cur_ref[...]
        mine = columns.at[iteration, x]
        pending = exchange([
            pltpu.make_async_remote_copy(
                src_ref=mine, dst_ref=mine,
                send_sem=col_send.at[iteration, j], recv_sem=col_recv.at[iteration, j],
                device_id=(r, (x + j) % nx), device_id_type=MESH,
            )
            for j in range(1, nx)
        ])
        every = jnp.concatenate([columns[iteration, j][:col_width] for j in range(nx)], 0)
        partial = lax.dot_general(
            every, every, (((1,), (1,)), ((), ())),
            precision=lax.Precision.HIGHEST, preferred_element_type=jnp.float32,
        )
        gram_a[iteration, my_place, :, 0:K] = partial
        mine_a = gram_a.at[iteration, my_place]
        pending += exchange([
            pltpu.make_async_remote_copy(
                src_ref=mine_a, dst_ref=mine_a,
                send_sem=a_send.at[iteration, j], recv_sem=a_recv.at[iteration, j],
                device_id=(my_group * group + (my_place + j) % group, x), device_id_type=MESH,
            )
            for j in range(1, group)
        ])
        gram_b[iteration, my_group] = sum(gram_a[iteration, j] for j in range(group))
        mine_b = gram_b.at[iteration, my_group]
        pending += exchange([
            pltpu.make_async_remote_copy(
                src_ref=mine_b, dst_ref=mine_b,
                send_sem=b_send.at[iteration, j], recv_sem=b_recv.at[iteration, j],
                device_id=((my_group + j) % n_groups * group + my_place, x), device_id_type=MESH,
            )
            for j in range(1, n_groups)
        ])
        gram = sum(gram_b[iteration, j] for j in range(n_groups)) / total_points
        row = lax.broadcasted_iota(jnp.int32, (K, TILE), 0)
        lane = lax.broadcasted_iota(jnp.int32, (K, TILE), 1)
        inverse = jnp.where(row == lane, 1.0, 0.0)
        for j in range(K - 1):
            factor = jnp.where(row > j, gram[:, j : j + 1] / gram[j : j + 1, j : j + 1], 0.0)
            inverse = inverse - factor * inverse[j : j + 1]
            gram = gram - factor * gram[j : j + 1]
        pivots = jnp.sum(jnp.where(row == lane, gram, 0.0), axis=1, keepdims=True)
        inverse = inverse * lax.rsqrt(pivots)
        combined = jnp.dot(
            mixing_ref[iteration, x], inverse,
            precision=lax.Precision.HIGHEST, preferred_element_type=jnp.float32,
        )
        vectors = jnp.dot(
            combined[:, :K], every,
            precision=lax.Precision.HIGHEST, preferred_element_type=jnp.float32,
        )
        prev_ref[...] = vectors
        cur_ref[...] = vectors
        for copy in pending:
            copy.wait_send()

    def one_iteration(iteration, carry):
        def one_order(order, inner):
            apply(iteration, order)
            return inner

        lax.fori_loop(0, DEGREE, one_order, 0)
        orthonormalize(iteration)
        return carry

    lax.fori_loop(0, ITERS, one_iteration, 0)
    out_ref[...] = cur_ref[...]


def body(start, weights, block_count, col_ids, send_ids, mixing):
    tiles = weights.shape[0]
    col_width, points = start.shape
    n, nx = lax.axis_size("rows"), lax.axis_size("cols")
    group = 4 if n % 4 == 0 else 1
    pad = SUB - col_width
    mixing = mixing.reshape(ITERS, nx, col_width, K)
    if pad:
        start = jnp.pad(start, ((0, pad), (0, 0)))
        mixing = jnp.pad(mixing, ((0, 0), (0, 0), (0, pad), (0, 0)))
    steps = ITERS * DEGREE
    vmem = pl.BlockSpec(memory_space=pltpu.VMEM)
    smem = pl.BlockSpec(memory_space=pltpu.SMEM)
    dma = pltpu.SemaphoreType.DMA
    out = pl.pallas_call(
        functools.partial(kernel, n, nx, group, col_width, tiles, float(points * n)),
        out_shape=jax.ShapeDtypeStruct((SUB, points), jnp.float32),
        in_specs=[smem, smem, smem, vmem, vmem, pl.BlockSpec(memory_space=pl.ANY)],
        out_specs=vmem,
        scratch_shapes=[
            pltpu.VMEM(weights.shape, jnp.bfloat16),
            pltpu.VMEM((SUB, points), jnp.float32),
            pltpu.VMEM((SUB, points), jnp.float32),
            pltpu.VMEM((SUB, points), jnp.float32),
            pltpu.VMEM((tiles + 2 * REACH * SLOTS + 1, SUB, TILE), jnp.float32),
            pltpu.VMEM((steps, 2 * REACH, SLOTS * SUB, TILE), jnp.bfloat16),
            pltpu.VMEM((steps, 2 * REACH, SLOTS * SUB, TILE), jnp.bfloat16),
            pltpu.VMEM((ITERS, nx, SUB, points), jnp.float32),
            pltpu.VMEM((ITERS, group, K, TILE), jnp.float32),
            pltpu.VMEM((ITERS, n // group, K, TILE), jnp.float32),
            dma((tiles,)),
            dma((steps, 2 * REACH)),
            dma((steps, 2 * REACH)),
            dma((ITERS, nx)),
            dma((ITERS, nx)),
            dma((ITERS, group)),
            dma((ITERS, group)),
            dma((ITERS, n // group)),
            dma((ITERS, n // group)),
        ],
        compiler_params=pltpu.CompilerParams(
            collective_id=0, has_side_effects=True, vmem_limit_bytes=32 * 1024 * 1024
        ),
    )(block_count, col_ids, send_ids, start, mixing, weights)
    return out[:col_width]


def solution(mesh):
    in_specs = (
        P("cols", "rows"),
        P("rows", None, None, None),
        P("rows"),
        P("rows", None),
        P("rows", None),
        P(),
    )
    out_specs = P("cols", "rows")
    return jax.shard_map(body, mesh=mesh, in_specs=in_specs, out_specs=out_specs, check_vma=False)
```

```python
import functools

import jax
import jax.numpy as jnp
from jax import lax
from jax.experimental import pallas as pl
from jax.experimental.pallas import tpu as pltpu
from jax.sharding import PartitionSpec as P

K = 16
NB = 8
REACH = 2
SLOTS = 2
DEGREE = 4
ITERS = 2
SUB = 8
TILE = 128

filter_center = 1.2
filter_half = 0.8

MESH = pl.DeviceIdType.MESH
DISTANCES = [p - REACH if p < REACH else p - REACH + 1 for p in range(2 * REACH)]


def kernel(
    n, nx, group, col_width, tiles, total_points,
    count_hbm, col_hbm, send_hbm, start_hbm, mixing_hbm, weights_hbm,
    out_ref,
    block_count, col_ids, send_ids, mixing_ref,
    w_ref, scale_ref, prev_ref, cur_ref, buf, outgoing, incoming, columns, gram_a, gram_b,
    w_sem, small_sem, send_sem, recv_sem, col_send, col_recv, a_send, a_recv, b_send, b_recv,
):
    r = lax.axis_index("rows")
    x = lax.axis_index("cols")
    n_groups = n // group
    my_group, my_place = r // group, r % group

    smalls = [
        pltpu.make_async_copy(src, dst, small_sem.at[i])
        for i, (src, dst) in enumerate((
            (count_hbm, block_count), (col_hbm, col_ids), (send_hbm, send_ids),
            (mixing_hbm, mixing_ref), (start_hbm, columns.at[x]),
        ))
    ]
    loads = [pltpu.make_async_copy(weights_hbm.at[t], w_ref.at[t], w_sem.at[t]) for t in range(tiles)]
    for load in smalls + loads:
        load.start()
    buf[tiles:] = jnp.zeros((buf.shape[0] - tiles, K, TILE), jnp.bfloat16)
    gram_a[...] = jnp.zeros_like(gram_a)

    barrier = pltpu.get_barrier_semaphore()
    greeted = (nx - 1) + (group - 1) + (n_groups - 1)
    for d in DISTANCES:
        reach = jnp.logical_and(r + d >= 0, r + d < n)

        @pl.when(reach)
        def _():
            pl.semaphore_signal(barrier, inc=1, device_id=(r + d, x), device_id_type=MESH)

        greeted = greeted + reach.astype(jnp.int32)
    for j in range(1, nx):
        pl.semaphore_signal(barrier, inc=1, device_id=(r, (x + j) % nx), device_id_type=MESH)
    for j in range(1, group):
        pl.semaphore_signal(
            barrier, inc=1, device_id=(my_group * group + (my_place + j) % group, x), device_id_type=MESH
        )
    for j in range(1, n_groups):
        pl.semaphore_signal(
            barrier, inc=1, device_id=((my_group + j) % n_groups * group + my_place, x), device_id_type=MESH
        )

    pl.semaphore_wait(barrier, greeted)
    column_copies = [
        pltpu.make_async_remote_copy(
            src_ref=start_hbm, dst_ref=columns.at[x], send_sem=col_send.at[j], recv_sem=col_recv.at[j],
            device_id=(r, (x + j) % nx), device_id_type=MESH,
        )
        for j in range(1, nx)
    ]
    for copy in column_copies:
        copy.start()

    def times_tile(t, blocks):
        w = jnp.concatenate([w_ref[t, b] for b in range(NB)], 1)
        return lax.dot_general(
            blocks, w, (((1,), (1,)), ((), ())), preferred_element_type=jnp.float32
        )

    for small in smalls:
        small.wait()
    for t in range(tiles):
        loads[t].wait()
        ones = [
            jnp.full((K, TILE), jnp.where(b < block_count[t], 1.0, 0.0), jnp.float32) for b in range(NB)
        ]
        degree = 1.0 + times_tile(t, jnp.concatenate(ones, 1).astype(jnp.bfloat16))
        scale_ref[:, t * TILE : (t + 1) * TILE] = lax.rsqrt(degree)
    for copy in column_copies:
        copy.wait()
    every_start = jnp.concatenate([columns[j][:col_width] for j in range(nx)], 0)
    prev_ref[...] = every_start
    cur_ref[...] = every_start

    def neighbour_copy(step, o):
        return pltpu.make_async_remote_copy(
            src_ref=outgoing.at[step, o],
            dst_ref=incoming.at[step, o],
            send_sem=send_sem.at[step, o],
            recv_sem=recv_sem.at[step, o],
            device_id=(r + DISTANCES[o], x),
            device_id_type=MESH,
        )

    def apply(iteration, order):
        step = iteration * DEGREE + order
        for t in range(tiles):
            at = slice(t * TILE, (t + 1) * TILE)
            scaled = (scale_ref[:, at] * cur_ref[:, at]).astype(jnp.bfloat16)
            buf[t] = scaled
        for o, d in enumerate(DISTANCES):
            for s in range(SLOTS):
                outgoing[step, o, s] = buf[send_ids[s, o]]

            @pl.when(jnp.logical_and(r + d >= 0, r + d < n))
            def _():
                neighbour_copy(step, o).start()

        for o, d in enumerate(DISTANCES):

            @pl.when(jnp.logical_and(r - d >= 0, r - d < n))
            def _():
                neighbour_copy(step, o).wait_recv()
                buf[tiles + o * SLOTS : tiles + (o + 1) * SLOTS] = incoming[step, o]

        first = order == 0
        gain = jnp.where(first, 1.0 / filter_half, 2.0 / filter_half)
        keep = jnp.where(first, 0.0, 1.0)
        empty = tiles + 2 * REACH * SLOTS
        for t in range(tiles):
            at = slice(t * TILE, (t + 1) * TILE)
            count = block_count[t]
            blocks = [buf[jnp.where(b < count, col_ids[b, t], empty)] for b in range(NB)]
            product = times_tile(t, jnp.concatenate(blocks, 1))
            current = cur_ref[:, at]
            laplacian = current - scale_ref[:, at] * (product + buf[t].astype(jnp.float32))
            following = gain * (laplacian - filter_center * current) - keep * prev_ref[:, at]
            prev_ref[:, at] = current
            cur_ref[:, at] = following
        for o, d in enumerate(DISTANCES):

            @pl.when(jnp.logical_and(r + d >= 0, r + d < n))
            def _():
                neighbour_copy(step, o).wait_send()

    def exchange(copies):
        for copy in copies:
            copy.start()
        for copy in copies:
            copy.wait_recv()
        return copies

    def orthonormalize(iteration):
        every = cur_ref[...]
        partial = lax.dot_general(
            every, every, (((1,), (1,)), ((), ())),
            precision=lax.Precision.HIGHEST, preferred_element_type=jnp.float32,
        )
        gram_a[iteration, my_place, :, 0:K] = partial
        mine_a = gram_a.at[iteration, my_place]
        pending = exchange([
            pltpu.make_async_remote_copy(
                src_ref=mine_a, dst_ref=mine_a,
                send_sem=a_send.at[iteration, j], recv_sem=a_recv.at[iteration, j],
                device_id=(my_group * group + (my_place + j) % group, x), device_id_type=MESH,
            )
            for j in range(1, group)
        ])
        gram_b[iteration, my_group] = sum(gram_a[iteration, j] for j in range(group))
        mine_b = gram_b.at[iteration, my_group]
        pending += exchange([
            pltpu.make_async_remote_copy(
                src_ref=mine_b, dst_ref=mine_b,
                send_sem=b_send.at[iteration, j], recv_sem=b_recv.at[iteration, j],
                device_id=((my_group + j) % n_groups * group + my_place, x), device_id_type=MESH,
            )
            for j in range(1, n_groups)
        ])
        gram = sum(gram_b[iteration, j] for j in range(n_groups)) / total_points
        row = lax.broadcasted_iota(jnp.int32, (K, TILE), 0)
        lane = lax.broadcasted_iota(jnp.int32, (K, TILE), 1)
        inverse = jnp.where(row == lane, 1.0, 0.0)
        for j in range(K - 1):
            factor = jnp.where(row > j, gram[:, j : j + 1] / gram[j : j + 1, j : j + 1], 0.0)
            inverse = inverse - factor * inverse[j : j + 1]
            gram = gram - factor * gram[j : j + 1]
        pivots = jnp.sum(jnp.where(row == lane, gram, 0.0), axis=1, keepdims=True)
        inverse = inverse * lax.rsqrt(pivots)
        combined = jnp.dot(
            mixing_ref[iteration], inverse,
            precision=lax.Precision.HIGHEST, preferred_element_type=jnp.float32,
        )
        vectors = jnp.dot(
            combined[:, :K], every,
            precision=lax.Precision.HIGHEST, preferred_element_type=jnp.float32,
        )
        prev_ref[...] = vectors
        cur_ref[...] = vectors
        for copy in pending:
            copy.wait_send()

    def one_iteration(iteration, carry):
        def one_order(order, inner):
            apply(iteration, order)
            return inner

        lax.fori_loop(0, DEGREE, one_order, 0)
        orthonormalize(iteration)
        return carry

    lax.fori_loop(0, ITERS, one_iteration, 0)
    for j in range(nx):

        @pl.when(x == j)
        def _():
            out_ref[...] = cur_ref[j * col_width : (j + 1) * col_width]


def body(start, weights, block_count, col_ids, send_ids, mixing):
    tiles = weights.shape[0]
    col_width, points = start.shape
    n, nx = lax.axis_size("rows"), lax.axis_size("cols")
    group = 4 if n % 4 == 0 else 1
    pad = SUB - col_width
    if pad:
        start = jnp.pad(start, ((0, pad), (0, 0)))
    steps = ITERS * DEGREE
    vmem = pl.BlockSpec(memory_space=pltpu.VMEM)
    dma = pltpu.SemaphoreType.DMA
    out = pl.pallas_call(
        functools.partial(kernel, n, nx, group, col_width, tiles, float(points * n)),
        out_shape=jax.ShapeDtypeStruct((col_width, points), jnp.float32),
        in_specs=[pl.BlockSpec(memory_space=pl.ANY)] * 6,
        out_specs=vmem,
        scratch_shapes=[
            pltpu.SMEM(block_count.shape, jnp.int32),
            pltpu.SMEM(col_ids.shape[::-1], jnp.int32),
            pltpu.SMEM(send_ids.shape[::-1], jnp.int32),
            pltpu.VMEM(mixing.shape, jnp.float32),
            pltpu.VMEM(weights.shape, jnp.bfloat16),
            pltpu.VMEM((K, points), jnp.float32),
            pltpu.VMEM((K, points), jnp.float32),
            pltpu.VMEM((K, points), jnp.float32),
            pltpu.VMEM((tiles + 2 * REACH * SLOTS + 1, K, TILE), jnp.bfloat16),
            pltpu.VMEM((steps, 2 * REACH, SLOTS, K, TILE), jnp.bfloat16),
            pltpu.VMEM((steps, 2 * REACH, SLOTS, K, TILE), jnp.bfloat16),
            pltpu.VMEM((nx, SUB, points), jnp.float32),
            pltpu.VMEM((ITERS, group, K, TILE), jnp.float32),
            pltpu.VMEM((ITERS, n // group, K, TILE), jnp.float32),
            dma((tiles,)),
            dma((5,)),
            dma((steps, 2 * REACH)),
            dma((steps, 2 * REACH)),
            dma((nx,)),
            dma((nx,)),
            dma((ITERS, group)),
            dma((ITERS, group)),
            dma((ITERS, n // group)),
            dma((ITERS, n // group)),
        ],
        compiler_params=pltpu.CompilerParams(
            collective_id=0, has_side_effects=True, vmem_limit_bytes=56 * 1024 * 1024
        ),
    )(block_count, col_ids.T, send_ids.T, start, mixing, weights)
    return out


def solution(mesh):
    in_specs = (
        P("cols", "rows"),
        P("rows", None, None, None),
        P("rows"),
        P("rows", None),
        P("rows", None),
        P(),
    )
    out_specs = P("cols", "rows")
    return jax.shard_map(body, mesh=mesh, in_specs=in_specs, out_specs=out_specs, check_vma=False)
```

```python
import functools

import jax
import jax.numpy as jnp
from jax import lax
from jax.experimental import pallas as pl
from jax.experimental.pallas import tpu as pltpu
from jax.sharding import PartitionSpec as P

K = 16
NB = 8
REACH = 2
SLOTS = 2
DEGREE = 4
ITERS = 2
SUB = 8
TILE = 128

filter_center = 1.2
filter_half = 0.8

MESH = pl.DeviceIdType.MESH
DISTANCES = [p - REACH if p < REACH else p - REACH + 1 for p in range(2 * REACH)]


def kernel(
    n, nx, group, col_width, tiles, total_points,
    count_hbm, col_hbm, send_hbm, start_hbm, mixing_hbm, weights_hbm,
    out_ref,
    block_count, col_ids, send_ids, mixing_ref,
    w_ref, scale_ref, prev_ref, cur_ref, buf, outgoing, incoming, columns, gram_a, gram_b,
    w_sem, small_sem, send_sem, recv_sem, col_send, col_recv, a_send, a_recv, b_send, b_recv,
):
    r = lax.axis_index("rows")
    x = lax.axis_index("cols")
    n_groups = n // group
    my_group, my_place = r // group, r % group

    smalls = [
        pltpu.make_async_copy(src, dst, small_sem.at[i])
        for i, (src, dst) in enumerate((
            (count_hbm, block_count), (col_hbm, col_ids), (send_hbm, send_ids),
            (mixing_hbm, mixing_ref), (start_hbm, columns.at[x]),
        ))
    ]
    loads = [pltpu.make_async_copy(weights_hbm.at[t], w_ref.at[t], w_sem.at[t]) for t in range(tiles)]
    for load in smalls + loads:
        load.start()
    buf[tiles:] = jnp.zeros((buf.shape[0] - tiles, K, TILE), jnp.bfloat16)
    gram_a[...] = jnp.zeros_like(gram_a)
    gram_b[...] = jnp.zeros_like(gram_b)

    barrier = pltpu.get_barrier_semaphore()
    greeted = (nx - 1) + (group - 1) + (n_groups - 1)
    for d in DISTANCES:
        reach = jnp.logical_and(r + d >= 0, r + d < n)

        @pl.when(reach)
        def _():
            pl.semaphore_signal(barrier, inc=1, device_id=(r + d, x), device_id_type=MESH)

        greeted = greeted + reach.astype(jnp.int32)
    for j in range(1, nx):
        pl.semaphore_signal(barrier, inc=1, device_id=(r, (x + j) % nx), device_id_type=MESH)
    for j in range(1, group):
        pl.semaphore_signal(
            barrier, inc=1, device_id=(my_group * group + (my_place + j) % group, x), device_id_type=MESH
        )
    for j in range(1, n_groups):
        pl.semaphore_signal(
            barrier, inc=1, device_id=((my_group + j) % n_groups * group + my_place, x), device_id_type=MESH
        )

    pl.semaphore_wait(barrier, greeted)
    column_copies = [
        pltpu.make_async_remote_copy(
            src_ref=start_hbm, dst_ref=columns.at[x], send_sem=col_send.at[j], recv_sem=col_recv.at[j],
            device_id=(r, (x + j) % nx), device_id_type=MESH,
        )
        for j in range(1, nx)
    ]
    for copy in column_copies:
        copy.start()

    def times_tile(t, blocks):
        w = jnp.concatenate([w_ref[t, b] for b in range(NB)], 1)
        return lax.dot_general(
            blocks, w, (((1,), (1,)), ((), ())), preferred_element_type=jnp.float32
        )

    for small in smalls:
        small.wait()
    for t in range(tiles):
        loads[t].wait()
        ones = [
            jnp.full((K, TILE), jnp.where(b < block_count[t], 1.0, 0.0), jnp.float32) for b in range(NB)
        ]
        degree = 1.0 + times_tile(t, jnp.concatenate(ones, 1).astype(jnp.bfloat16))
        scale_ref[:, t * TILE : (t + 1) * TILE] = lax.rsqrt(degree)
    for copy in column_copies:
        copy.wait()
    every_start = jnp.concatenate([columns[j][:col_width] for j in range(nx)], 0)
    prev_ref[...] = every_start
    cur_ref[...] = every_start

    def neighbour_copy(step, o):
        return pltpu.make_async_remote_copy(
            src_ref=outgoing.at[step, o],
            dst_ref=incoming.at[step, o],
            send_sem=send_sem.at[step, o],
            recv_sem=recv_sem.at[step, o],
            device_id=(r + DISTANCES[o], x),
            device_id_type=MESH,
        )

    def apply(step, order):
        for t in range(tiles):
            at = slice(t * TILE, (t + 1) * TILE)
            scaled = (scale_ref[:, at] * cur_ref[:, at]).astype(jnp.bfloat16)
            buf[t] = scaled
        for o, d in enumerate(DISTANCES):
            for s in range(SLOTS):
                outgoing[step, o, s] = buf[send_ids[s, o]]

            @pl.when(jnp.logical_and(r + d >= 0, r + d < n))
            def _():
                neighbour_copy(step, o).start()

        for o, d in enumerate(DISTANCES):

            @pl.when(jnp.logical_and(r - d >= 0, r - d < n))
            def _():
                neighbour_copy(step, o).wait_recv()
                buf[tiles + o * SLOTS : tiles + (o + 1) * SLOTS] = incoming[step, o]

        first = jnp.equal(order, 0)
        gain = jnp.where(first, 1.0 / filter_half, 2.0 / filter_half)
        keep = jnp.where(first, 0.0, 1.0)
        empty = tiles + 2 * REACH * SLOTS
        for t in range(tiles):
            at = slice(t * TILE, (t + 1) * TILE)
            count = block_count[t]
            blocks = [buf[jnp.where(b < count, col_ids[b, t], empty)] for b in range(NB)]
            product = times_tile(t, jnp.concatenate(blocks, 1))
            current = cur_ref[:, at]
            laplacian = current - scale_ref[:, at] * (product + buf[t].astype(jnp.float32))
            following = gain * (laplacian - filter_center * current) - keep * prev_ref[:, at]
            prev_ref[:, at] = current
            cur_ref[:, at] = following
        for o, d in enumerate(DISTANCES):

            @pl.when(jnp.logical_and(r + d >= 0, r + d < n))
            def _():
                neighbour_copy(step, o).wait_send()

    def group_copies(iteration):
        mine = gram_a.at[iteration, my_place]
        return [
            pltpu.make_async_remote_copy(
                src_ref=mine, dst_ref=mine,
                send_sem=a_send.at[iteration, j], recv_sem=a_recv.at[iteration, j],
                device_id=(my_group * group + (my_place + j) % group, x), device_id_type=MESH,
            )
            for j in range(1, group)
        ]

    def across_copies(iteration):
        mine = gram_b.at[iteration, my_group]
        return [
            pltpu.make_async_remote_copy(
                src_ref=mine, dst_ref=mine,
                send_sem=b_send.at[iteration, j], recv_sem=b_recv.at[iteration, j],
                device_id=((my_group + j) % n_groups * group + my_place, x), device_id_type=MESH,
            )
            for j in range(1, n_groups)
        ]

    def start_gram(iteration):
        every = cur_ref[...]
        partial = lax.dot_general(
            every, every, (((1,), (1,)), ((), ())),
            precision=lax.Precision.HIGHEST, preferred_element_type=jnp.float32,
        )
        gram_a[iteration, my_place, :, 0:K] = partial[:SUB]
        gram_a[iteration, my_place, :, K : 2 * K] = partial[SUB:]
        pending = group_copies(iteration)
        for copy in pending:
            copy.start()
        for copy in pending:
            copy.wait()
        gram_b[iteration, my_group] = sum(gram_a[iteration, j] for j in range(group))
        pending = across_copies(iteration)
        for copy in pending:
            copy.start()
        return pending

    def finish_gram(iteration, pending):
        for copy in pending:
            copy.wait_recv()
        packed = sum(gram_b[iteration, j] for j in range(n_groups)) / total_points
        gram = jnp.concatenate([packed[:, :K], packed[:, K : 2 * K]], 0)
        row = lax.broadcasted_iota(jnp.int32, (K, K), 0)
        lane = lax.broadcasted_iota(jnp.int32, (K, K), 1)
        inverse = jnp.where(row == lane, 1.0, 0.0)
        for j in range(K - 1):
            factor = jnp.where(row > j, gram[:, j : j + 1] / gram[j : j + 1, j : j + 1], 0.0)
            inverse = inverse - factor * inverse[j : j + 1]
            gram = gram - factor * gram[j : j + 1]
        pivots = jnp.sum(jnp.where(row == lane, gram, 0.0), axis=1, keepdims=True)
        inverse = inverse * lax.rsqrt(pivots)
        return jnp.dot(
            mixing_ref[iteration], inverse,
            precision=lax.Precision.HIGHEST, preferred_element_type=jnp.float32,
        )

    def mixed(combined, vectors):
        return jnp.dot(
            combined, vectors,
            precision=lax.Precision.HIGHEST, preferred_element_type=jnp.float32,
        )

    def one_step(step, carry):
        apply(step, step % DEGREE)
        return carry

    lax.fori_loop(0, DEGREE, one_step, 0)
    for iteration in range(ITERS):
        pending = start_gram(iteration)
        if iteration < ITERS - 1:
            apply((iteration + 1) * DEGREE, 0)
            combined = finish_gram(iteration, pending)
            prev_ref[...] = mixed(combined, prev_ref[...])
            cur_ref[...] = mixed(combined, cur_ref[...])
            lax.fori_loop((iteration + 1) * DEGREE + 1, (iteration + 2) * DEGREE, one_step, 0)
        else:
            combined = finish_gram(iteration, pending)
            for j in range(nx):

                @pl.when(x == j)
                def _():
                    out_ref[...] = mixed(combined[j * col_width : (j + 1) * col_width], cur_ref[...])

        for copy in pending:
            copy.wait_send()


def body(start, weights, block_count, col_ids, send_ids, mixing):
    tiles = weights.shape[0]
    col_width, points = start.shape
    n, nx = lax.axis_size("rows"), lax.axis_size("cols")
    group = 4 if n > 16 and n % 4 == 0 else 1
    pad = SUB - col_width
    if pad:
        start = jnp.pad(start, ((0, pad), (0, 0)))
    steps = ITERS * DEGREE
    vmem = pl.BlockSpec(memory_space=pltpu.VMEM)
    dma = pltpu.SemaphoreType.DMA
    out = pl.pallas_call(
        functools.partial(kernel, n, nx, group, col_width, tiles, float(points * n)),
        out_shape=jax.ShapeDtypeStruct((col_width, points), jnp.float32),
        in_specs=[pl.BlockSpec(memory_space=pl.ANY)] * 6,
        out_specs=vmem,
        scratch_shapes=[
            pltpu.SMEM(block_count.shape, jnp.int32),
            pltpu.SMEM(col_ids.shape[::-1], jnp.int32),
            pltpu.SMEM(send_ids.shape[::-1], jnp.int32),
            pltpu.VMEM(mixing.shape, jnp.float32),
            pltpu.VMEM(weights.shape, jnp.bfloat16),
            pltpu.VMEM((K, points), jnp.float32),
            pltpu.VMEM((K, points), jnp.float32),
            pltpu.VMEM((K, points), jnp.float32),
            pltpu.VMEM((tiles + 2 * REACH * SLOTS + 1, K, TILE), jnp.bfloat16),
            pltpu.VMEM((steps, 2 * REACH, SLOTS, K, TILE), jnp.bfloat16),
            pltpu.VMEM((steps, 2 * REACH, SLOTS, K, TILE), jnp.bfloat16),
            pltpu.VMEM((nx, SUB, points), jnp.float32),
            pltpu.VMEM((ITERS, group, SUB, TILE), jnp.float32),
            pltpu.VMEM((ITERS, n // group, SUB, TILE), jnp.float32),
            dma((tiles,)),
            dma((5,)),
            dma((steps, 2 * REACH)),
            dma((steps, 2 * REACH)),
            dma((nx,)),
            dma((nx,)),
            dma((ITERS, group)),
            dma((ITERS, group)),
            dma((ITERS, n // group)),
            dma((ITERS, n // group)),
        ],
        compiler_params=pltpu.CompilerParams(
            collective_id=0, has_side_effects=True, vmem_limit_bytes=56 * 1024 * 1024
        ),
    )(block_count, col_ids.T, send_ids.T, start, mixing, weights)
    return out


def solution(mesh):
    in_specs = (
        P("cols", "rows"),
        P("rows", None, None, None),
        P("rows"),
        P("rows", None),
        P("rows", None),
        P(),
    )
    out_specs = P("cols", "rows")
    return jax.shard_map(body, mesh=mesh, in_specs=in_specs, out_specs=out_specs, check_vma=False)
```

```python
import functools

import jax
import jax.numpy as jnp
from jax import lax
from jax.experimental import pallas as pl
from jax.experimental.pallas import tpu as pltpu
from jax.sharding import PartitionSpec as P

K = 16
NB = 8
REACH = 2
SLOTS = 2
DEGREE = 4
ITERS = 2
SUB = 8
TILE = 128

filter_center = 1.2
filter_half = 0.8

MESH = pl.DeviceIdType.MESH
DISTANCES = [p - REACH if p < REACH else p - REACH + 1 for p in range(2 * REACH)]


def kernel(
    n, nx, group, col_width, tiles, total_points,
    count_hbm, col_hbm, send_hbm, start_hbm, mixing_hbm, weights_hbm,
    out_ref,
    block_count, col_ids, send_ids, sources, mixing_ref,
    w_ref, scale_ref, prev_ref, cur_ref, buf, outgoing, incoming, columns, gram_a, gram_b,
    w_sem, small_sem, send_sem, recv_sem, col_send, col_recv, a_send, a_recv, b_send, b_recv,
):
    r = lax.axis_index("rows")
    x = lax.axis_index("cols")
    n_groups = n // group
    my_group, my_place = r // group, r % group

    smalls = [
        pltpu.make_async_copy(src, dst, small_sem.at[i])
        for i, (src, dst) in enumerate((
            (count_hbm, block_count), (col_hbm, col_ids), (send_hbm, send_ids),
            (mixing_hbm, mixing_ref), (start_hbm, columns.at[x]),
        ))
    ]
    loads = [pltpu.make_async_copy(weights_hbm.at[t], w_ref.at[t], w_sem.at[t]) for t in range(tiles)]
    for load in smalls + loads:
        load.start()
    buf[:, tiles:] = jnp.zeros((2, buf.shape[1] - tiles, K, TILE), jnp.bfloat16)
    gram_a[...] = jnp.zeros_like(gram_a)
    gram_b[...] = jnp.zeros_like(gram_b)

    barrier = pltpu.get_barrier_semaphore()
    greeted = (nx - 1) + (group - 1) + (n_groups - 1)
    for d in DISTANCES:
        reach = jnp.logical_and(r + d >= 0, r + d < n)

        @pl.when(reach)
        def _():
            pl.semaphore_signal(barrier, inc=1, device_id=(r + d, x), device_id_type=MESH)

        greeted = greeted + reach.astype(jnp.int32)
    for j in range(1, nx):
        pl.semaphore_signal(barrier, inc=1, device_id=(r, (x + j) % nx), device_id_type=MESH)
    for j in range(1, group):
        pl.semaphore_signal(
            barrier, inc=1, device_id=(my_group * group + (my_place + j) % group, x), device_id_type=MESH
        )
    for j in range(1, n_groups):
        pl.semaphore_signal(
            barrier, inc=1, device_id=((my_group + j) % n_groups * group + my_place, x), device_id_type=MESH
        )

    pl.semaphore_wait(barrier, greeted)
    column_copies = [
        pltpu.make_async_remote_copy(
            src_ref=start_hbm, dst_ref=columns.at[x], send_sem=col_send.at[j], recv_sem=col_recv.at[j],
            device_id=(r, (x + j) % nx), device_id_type=MESH,
        )
        for j in range(1, nx)
    ]
    for copy in column_copies:
        copy.start()

    def times_tile(t, blocks):
        w = jnp.concatenate([w_ref[t, b] for b in range(NB)], 1)
        return lax.dot_general(
            blocks, w, (((1,), (1,)), ((), ())), preferred_element_type=jnp.float32
        )

    empty = tiles + 2 * REACH * SLOTS
    for small in smalls:
        small.wait()
    for t in range(tiles):
        loads[t].wait()
        for b in range(NB):
            sources[b, t] = jnp.where(b < block_count[t], col_ids[b, t], empty)
        ones = [
            jnp.full((K, TILE), jnp.where(b < block_count[t], 1.0, 0.0), jnp.float32) for b in range(NB)
        ]
        degree = 1.0 + times_tile(t, jnp.concatenate(ones, 1).astype(jnp.bfloat16))
        scale_ref[:, t * TILE : (t + 1) * TILE] = lax.rsqrt(degree)
    for copy in column_copies:
        copy.wait()
    every_start = jnp.concatenate([columns[j][:col_width] for j in range(nx)], 0)
    prev_ref[...] = every_start
    cur_ref[...] = every_start

    def neighbour_copy(step, o):
        return pltpu.make_async_remote_copy(
            src_ref=outgoing.at[step, o],
            dst_ref=incoming.at[step, o],
            send_sem=send_sem.at[step, o],
            recv_sem=recv_sem.at[step, o],
            device_id=(r + DISTANCES[o], x),
            device_id_type=MESH,
        )

    def rescale(slot):
        for t in range(tiles):
            at = slice(t * TILE, (t + 1) * TILE)
            buf[slot, t] = (scale_ref[:, at] * cur_ref[:, at]).astype(jnp.bfloat16)

    def apply(step, order):
        now = step % 2
        later = 1 - now
        for o, d in enumerate(DISTANCES):
            for s in range(SLOTS):
                outgoing[step, o, s] = buf[now, send_ids[s, o]]

            @pl.when(jnp.logical_and(r + d >= 0, r + d < n))
            def _():
                neighbour_copy(step, o).start()

        for o, d in enumerate(DISTANCES):

            @pl.when(jnp.logical_and(r - d >= 0, r - d < n))
            def _():
                neighbour_copy(step, o).wait_recv()
                buf[now, tiles + o * SLOTS : tiles + (o + 1) * SLOTS] = incoming[step, o]

        first = jnp.equal(order, 0)
        gain = jnp.where(first, 1.0 / filter_half, 2.0 / filter_half)
        keep = jnp.where(first, 0.0, 1.0)
        for t in range(tiles):
            at = slice(t * TILE, (t + 1) * TILE)
            blocks = [buf[now, sources[b, t]] for b in range(NB)]
            product = times_tile(t, jnp.concatenate(blocks, 1))
            current = cur_ref[:, at]
            laplacian = current - scale_ref[:, at] * (product + buf[now, t].astype(jnp.float32))
            following = gain * (laplacian - filter_center * current) - keep * prev_ref[:, at]
            prev_ref[:, at] = current
            cur_ref[:, at] = following
            buf[later, t] = (scale_ref[:, at] * following).astype(jnp.bfloat16)

    def group_copies(iteration):
        mine = gram_a.at[iteration, my_place]
        return [
            pltpu.make_async_remote_copy(
                src_ref=mine, dst_ref=mine,
                send_sem=a_send.at[iteration, j], recv_sem=a_recv.at[iteration, j],
                device_id=(my_group * group + (my_place + j) % group, x), device_id_type=MESH,
            )
            for j in range(1, group)
        ]

    def across_copies(iteration):
        mine = gram_b.at[iteration, my_group]
        return [
            pltpu.make_async_remote_copy(
                src_ref=mine, dst_ref=mine,
                send_sem=b_send.at[iteration, j], recv_sem=b_recv.at[iteration, j],
                device_id=((my_group + j) % n_groups * group + my_place, x), device_id_type=MESH,
            )
            for j in range(1, n_groups)
        ]

    def start_gram(iteration):
        every = cur_ref[...]
        partial = lax.dot_general(
            every, every, (((1,), (1,)), ((), ())),
            precision=lax.Precision.HIGHEST, preferred_element_type=jnp.float32,
        )
        gram_a[iteration, my_place, :, 0:K] = partial[:SUB]
        gram_a[iteration, my_place, :, K : 2 * K] = partial[SUB:]
        pending = group_copies(iteration)
        for copy in pending:
            copy.start()
        for copy in pending:
            copy.wait()
        gram_b[iteration, my_group] = sum(gram_a[iteration, j] for j in range(group))
        pending = across_copies(iteration)
        for copy in pending:
            copy.start()
        return pending

    def finish_gram(iteration, pending):
        for copy in pending:
            copy.wait_recv()
        packed = sum(gram_b[iteration, j] for j in range(n_groups)) / total_points
        gram = jnp.concatenate([packed[:, :K], packed[:, K : 2 * K]], 0)
        row = lax.broadcasted_iota(jnp.int32, (K, K), 0)
        lane = lax.broadcasted_iota(jnp.int32, (K, K), 1)
        inverse = jnp.where(row == lane, 1.0, 0.0)
        for j in range(K - 1):
            factor = jnp.where(row > j, gram[:, j : j + 1] / gram[j : j + 1, j : j + 1], 0.0)
            inverse = inverse - factor * inverse[j : j + 1]
            gram = gram - factor * gram[j : j + 1]
        pivots = jnp.sum(jnp.where(row == lane, gram, 0.0), axis=1, keepdims=True)
        inverse = inverse * lax.rsqrt(pivots)
        return jnp.dot(
            mixing_ref[iteration], inverse,
            precision=lax.Precision.HIGHEST, preferred_element_type=jnp.float32,
        )

    def mixed(combined, vectors):
        return jnp.dot(
            combined, vectors,
            precision=lax.Precision.HIGHEST, preferred_element_type=jnp.float32,
        )

    def one_step(step, carry):
        apply(step, step % DEGREE)
        return carry

    rescale(0)
    lax.fori_loop(0, DEGREE, one_step, 0)
    for iteration in range(ITERS):
        pending = start_gram(iteration)
        if iteration < ITERS - 1:
            apply((iteration + 1) * DEGREE, 0)
            combined = finish_gram(iteration, pending)
            prev_ref[...] = mixed(combined, prev_ref[...])
            cur_ref[...] = mixed(combined, cur_ref[...])
            rescale(((iteration + 1) * DEGREE + 1) % 2)
            lax.fori_loop((iteration + 1) * DEGREE + 1, (iteration + 2) * DEGREE, one_step, 0)
        else:
            combined = finish_gram(iteration, pending)
            for j in range(nx):

                @pl.when(x == j)
                def _():
                    out_ref[...] = mixed(combined[j * col_width : (j + 1) * col_width], cur_ref[...])

        for copy in pending:
            copy.wait_send()

    def one_sent(step, carry):
        for o, d in enumerate(DISTANCES):

            @pl.when(jnp.logical_and(r + d >= 0, r + d < n))
            def _():
                neighbour_copy(step, o).wait_send()
        return carry

    lax.fori_loop(0, ITERS * DEGREE, one_sent, 0)


def body(start, weights, block_count, col_ids, send_ids, mixing):
    tiles = weights.shape[0]
    col_width, points = start.shape
    n, nx = lax.axis_size("rows"), lax.axis_size("cols")
    group = 4 if n > 16 and n % 4 == 0 else 1
    pad = SUB - col_width
    if pad:
        start = jnp.pad(start, ((0, pad), (0, 0)))
    steps = ITERS * DEGREE
    vmem = pl.BlockSpec(memory_space=pltpu.VMEM)
    dma = pltpu.SemaphoreType.DMA
    out = pl.pallas_call(
        functools.partial(kernel, n, nx, group, col_width, tiles, float(points * n)),
        out_shape=jax.ShapeDtypeStruct((col_width, points), jnp.float32),
        in_specs=[pl.BlockSpec(memory_space=pl.ANY)] * 6,
        out_specs=vmem,
        scratch_shapes=[
            pltpu.SMEM(block_count.shape, jnp.int32),
            pltpu.SMEM(col_ids.shape[::-1], jnp.int32),
            pltpu.SMEM(send_ids.shape[::-1], jnp.int32),
            pltpu.SMEM(col_ids.shape[::-1], jnp.int32),
            pltpu.VMEM(mixing.shape, jnp.float32),
            pltpu.VMEM(weights.shape, jnp.bfloat16),
            pltpu.VMEM((K, points), jnp.float32),
            pltpu.VMEM((K, points), jnp.float32),
            pltpu.VMEM((K, points), jnp.float32),
            pltpu.VMEM((2, tiles + 2 * REACH * SLOTS + 1, K, TILE), jnp.bfloat16),
            pltpu.VMEM((steps, 2 * REACH, SLOTS, K, TILE), jnp.bfloat16),
            pltpu.VMEM((steps, 2 * REACH, SLOTS, K, TILE), jnp.bfloat16),
            pltpu.VMEM((nx, SUB, points), jnp.float32),
            pltpu.VMEM((ITERS, group, SUB, TILE), jnp.float32),
            pltpu.VMEM((ITERS, n // group, SUB, TILE), jnp.float32),
            dma((tiles,)),
            dma((5,)),
            dma((steps, 2 * REACH)),
            dma((steps, 2 * REACH)),
            dma((nx,)),
            dma((nx,)),
            dma((ITERS, group)),
            dma((ITERS, group)),
            dma((ITERS, n // group)),
            dma((ITERS, n // group)),
        ],
        compiler_params=pltpu.CompilerParams(
            collective_id=0, has_side_effects=True, vmem_limit_bytes=56 * 1024 * 1024
        ),
    )(block_count, col_ids.T, send_ids.T, start, mixing, weights)
    return out


def solution(mesh):
    in_specs = (
        P("cols", "rows"),
        P("rows", None, None, None),
        P("rows"),
        P("rows", None),
        P("rows", None),
        P(),
    )
    out_specs = P("cols", "rows")
    return jax.shard_map(body, mesh=mesh, in_specs=in_specs, out_specs=out_specs, check_vma=False)
```

```python
import functools

import jax
import jax.numpy as jnp
from jax import lax
from jax.experimental import pallas as pl
from jax.experimental.pallas import tpu as pltpu
from jax.sharding import PartitionSpec as P

K = 16
NB = 8
REACH = 2
SLOTS = 2
DEGREE = 4
ITERS = 2
SUB = 8
TILE = 128

filter_center = 1.2
filter_half = 0.8

MESH = pl.DeviceIdType.MESH
DISTANCES = [p - REACH if p < REACH else p - REACH + 1 for p in range(2 * REACH)]


def kernel(
    n, nx, group, col_width, tiles, total_points,
    count_hbm, col_hbm, send_hbm, start_hbm, mixing_hbm, weights_hbm,
    out_ref,
    block_count, col_ids, send_ids, sources, mixing_ref,
    w_ref, scale_ref, prev_ref, cur_ref, buf, outgoing, incoming, columns, gram_a, gram_b,
    w_sem, small_sem, send_sem, recv_sem, col_send, col_recv, a_send, a_recv, b_send, b_recv,
):
    r = lax.axis_index("rows")
    x = lax.axis_index("cols")
    n_groups = n // group
    my_group, my_place = r // group, r % group

    smalls = [
        pltpu.make_async_copy(src, dst, small_sem.at[i])
        for i, (src, dst) in enumerate((
            (count_hbm, block_count), (col_hbm, col_ids), (send_hbm, send_ids),
            (mixing_hbm, mixing_ref), (start_hbm, columns.at[x]),
        ))
    ]
    loads = [pltpu.make_async_copy(weights_hbm.at[t], w_ref.at[t], w_sem.at[t]) for t in range(tiles)]
    for load in smalls + loads:
        load.start()
    buf[tiles:] = jnp.zeros((buf.shape[0] - tiles, K, TILE), jnp.bfloat16)
    gram_a[...] = jnp.zeros_like(gram_a)
    gram_b[...] = jnp.zeros_like(gram_b)

    barrier = pltpu.get_barrier_semaphore()
    greeted = (nx - 1) + (group - 1) + (n_groups - 1)
    for d in DISTANCES:
        reach = jnp.logical_and(r + d >= 0, r + d < n)

        @pl.when(reach)
        def _():
            pl.semaphore_signal(barrier, inc=1, device_id=(r + d, x), device_id_type=MESH)

        greeted = greeted + reach.astype(jnp.int32)
    for j in range(1, nx):
        pl.semaphore_signal(barrier, inc=1, device_id=(r, (x + j) % nx), device_id_type=MESH)
    for j in range(1, group):
        pl.semaphore_signal(
            barrier, inc=1, device_id=(my_group * group + (my_place + j) % group, x), device_id_type=MESH
        )
    for j in range(1, n_groups):
        pl.semaphore_signal(
            barrier, inc=1, device_id=((my_group + j) % n_groups * group + my_place, x), device_id_type=MESH
        )

    pl.semaphore_wait(barrier, greeted)
    column_copies = [
        pltpu.make_async_remote_copy(
            src_ref=start_hbm, dst_ref=columns.at[x], send_sem=col_send.at[j], recv_sem=col_recv.at[j],
            device_id=(r, (x + j) % nx), device_id_type=MESH,
        )
        for j in range(1, nx)
    ]
    for copy in column_copies:
        copy.start()

    def times_tile(t, blocks):
        w = jnp.concatenate([w_ref[t, b] for b in range(NB)], 1)
        return lax.dot_general(
            blocks, w, (((1,), (1,)), ((), ())), preferred_element_type=jnp.float32
        )

    empty = tiles + 2 * REACH * SLOTS
    for small in smalls:
        small.wait()
    for t in range(tiles):
        loads[t].wait()
        for b in range(NB):
            sources[b, t] = jnp.where(b < block_count[t], col_ids[b, t], empty)
        ones = [
            jnp.full((K, TILE), jnp.where(b < block_count[t], 1.0, 0.0), jnp.float32) for b in range(NB)
        ]
        degree = 1.0 + times_tile(t, jnp.concatenate(ones, 1).astype(jnp.bfloat16))
        scale_ref[:, t * TILE : (t + 1) * TILE] = lax.rsqrt(degree)
    for copy in column_copies:
        copy.wait()
    every_start = jnp.concatenate([columns[j][:col_width] for j in range(nx)], 0)
    prev_ref[...] = every_start
    cur_ref[...] = every_start

    def neighbour_copy(step, o):
        return pltpu.make_async_remote_copy(
            src_ref=outgoing.at[step, o],
            dst_ref=incoming.at[step, o],
            send_sem=send_sem.at[step, o],
            recv_sem=recv_sem.at[step, o],
            device_id=(r + DISTANCES[o], x),
            device_id_type=MESH,
        )

    def apply(step, order):
        for t in range(tiles):
            at = slice(t * TILE, (t + 1) * TILE)
            scaled = (scale_ref[:, at] * cur_ref[:, at]).astype(jnp.bfloat16)
            buf[t] = scaled
        for o, d in enumerate(DISTANCES):
            for s in range(SLOTS):
                outgoing[step, o, s] = buf[send_ids[s, o]]

            @pl.when(jnp.logical_and(r + d >= 0, r + d < n))
            def _():
                neighbour_copy(step, o).start()

        for o, d in enumerate(DISTANCES):

            @pl.when(jnp.logical_and(r - d >= 0, r - d < n))
            def _():
                neighbour_copy(step, o).wait_recv()
                buf[tiles + o * SLOTS : tiles + (o + 1) * SLOTS] = incoming[step, o]

        first = jnp.equal(order, 0)
        gain = jnp.where(first, 1.0 / filter_half, 2.0 / filter_half)
        keep = jnp.where(first, 0.0, 1.0)
        for t in range(tiles):
            at = slice(t * TILE, (t + 1) * TILE)
            blocks = [buf[sources[b, t]] for b in range(NB)]
            product = times_tile(t, jnp.concatenate(blocks, 1))
            current = cur_ref[:, at]
            laplacian = current - scale_ref[:, at] * (product + buf[t].astype(jnp.float32))
            following = gain * (laplacian - filter_center * current) - keep * prev_ref[:, at]
            prev_ref[:, at] = current
            cur_ref[:, at] = following

    def group_copies(iteration):
        mine = gram_a.at[iteration, my_place]
        return [
            pltpu.make_async_remote_copy(
                src_ref=mine, dst_ref=mine,
                send_sem=a_send.at[iteration, j], recv_sem=a_recv.at[iteration, j],
                device_id=(my_group * group + (my_place + j) % group, x), device_id_type=MESH,
            )
            for j in range(1, group)
        ]

    def across_copies(iteration):
        mine = gram_b.at[iteration, my_group]
        return [
            pltpu.make_async_remote_copy(
                src_ref=mine, dst_ref=mine,
                send_sem=b_send.at[iteration, j], recv_sem=b_recv.at[iteration, j],
                device_id=((my_group + j) % n_groups * group + my_place, x), device_id_type=MESH,
            )
            for j in range(1, n_groups)
        ]

    def start_gram(iteration):
        every = cur_ref[...]
        partial = lax.dot_general(
            every, every, (((1,), (1,)), ((), ())),
            precision=lax.Precision.HIGHEST, preferred_element_type=jnp.float32,
        )
        gram_a[iteration, my_place, :, 0:K] = partial[:SUB]
        gram_a[iteration, my_place, :, K : 2 * K] = partial[SUB:]
        pending = group_copies(iteration)
        for copy in pending:
            copy.start()
        for copy in pending:
            copy.wait()
        gram_b[iteration, my_group] = sum(gram_a[iteration, j] for j in range(group))
        pending = across_copies(iteration)
        for copy in pending:
            copy.start()
        return pending

    def finish_gram(iteration, pending):
        for copy in pending:
            copy.wait_recv()
        packed = sum(gram_b[iteration, j] for j in range(n_groups)) / total_points
        gram = jnp.concatenate([packed[:, :K], packed[:, K : 2 * K]], 0)
        row = lax.broadcasted_iota(jnp.int32, (K, K), 0)
        lane = lax.broadcasted_iota(jnp.int32, (K, K), 1)
        inverse = jnp.where(row == lane, 1.0, 0.0)
        for j in range(K - 1):
            factor = jnp.where(row > j, gram[:, j : j + 1] / gram[j : j + 1, j : j + 1], 0.0)
            inverse = inverse - factor * inverse[j : j + 1]
            gram = gram - factor * gram[j : j + 1]
        pivots = jnp.sum(jnp.where(row == lane, gram, 0.0), axis=1, keepdims=True)
        inverse = inverse * lax.rsqrt(pivots)
        return jnp.dot(
            mixing_ref[iteration], inverse,
            precision=lax.Precision.HIGHEST, preferred_element_type=jnp.float32,
        )

    def mixed(combined, vectors):
        return jnp.dot(
            combined, vectors,
            precision=lax.Precision.HIGHEST, preferred_element_type=jnp.float32,
        )

    def one_step(step, carry):
        apply(step, step % DEGREE)
        return carry

    lax.fori_loop(0, DEGREE, one_step, 0)
    for iteration in range(ITERS):
        pending = start_gram(iteration)
        if iteration < ITERS - 1:
            apply((iteration + 1) * DEGREE, 0)
            combined = finish_gram(iteration, pending)
            prev_ref[...] = mixed(combined, prev_ref[...])
            cur_ref[...] = mixed(combined, cur_ref[...])
            lax.fori_loop((iteration + 1) * DEGREE + 1, (iteration + 2) * DEGREE, one_step, 0)
        else:
            combined = finish_gram(iteration, pending)
            for j in range(nx):

                @pl.when(x == j)
                def _():
                    out_ref[...] = mixed(combined[j * col_width : (j + 1) * col_width], cur_ref[...])

        for copy in pending:
            copy.wait_send()

    def one_sent(step, carry):
        for o, d in enumerate(DISTANCES):

            @pl.when(jnp.logical_and(r + d >= 0, r + d < n))
            def _():
                neighbour_copy(step, o).wait_send()
        return carry

    lax.fori_loop(0, ITERS * DEGREE, one_sent, 0)


def body(start, weights, block_count, col_ids, send_ids, mixing):
    tiles = weights.shape[0]
    col_width, points = start.shape
    n, nx = lax.axis_size("rows"), lax.axis_size("cols")
    group = 4 if n > 16 and n % 4 == 0 else 1
    pad = SUB - col_width
    if pad:
        start = jnp.pad(start, ((0, pad), (0, 0)))
    steps = ITERS * DEGREE
    vmem = pl.BlockSpec(memory_space=pltpu.VMEM)
    dma = pltpu.SemaphoreType.DMA
    out = pl.pallas_call(
        functools.partial(kernel, n, nx, group, col_width, tiles, float(points * n)),
        out_shape=jax.ShapeDtypeStruct((col_width, points), jnp.float32),
        in_specs=[pl.BlockSpec(memory_space=pl.ANY)] * 6,
        out_specs=vmem,
        scratch_shapes=[
            pltpu.SMEM(block_count.shape, jnp.int32),
            pltpu.SMEM(col_ids.shape[::-1], jnp.int32),
            pltpu.SMEM(send_ids.shape[::-1], jnp.int32),
            pltpu.SMEM(col_ids.shape[::-1], jnp.int32),
            pltpu.VMEM(mixing.shape, jnp.float32),
            pltpu.VMEM(weights.shape, jnp.bfloat16),
            pltpu.VMEM((K, points), jnp.float32),
            pltpu.VMEM((K, points), jnp.float32),
            pltpu.VMEM((K, points), jnp.float32),
            pltpu.VMEM((tiles + 2 * REACH * SLOTS + 1, K, TILE), jnp.bfloat16),
            pltpu.VMEM((steps, 2 * REACH, SLOTS, K, TILE), jnp.bfloat16),
            pltpu.VMEM((steps, 2 * REACH, SLOTS, K, TILE), jnp.bfloat16),
            pltpu.VMEM((nx, SUB, points), jnp.float32),
            pltpu.VMEM((ITERS, group, SUB, TILE), jnp.float32),
            pltpu.VMEM((ITERS, n // group, SUB, TILE), jnp.float32),
            dma((tiles,)),
            dma((5,)),
            dma((steps, 2 * REACH)),
            dma((steps, 2 * REACH)),
            dma((nx,)),
            dma((nx,)),
            dma((ITERS, group)),
            dma((ITERS, group)),
            dma((ITERS, n // group)),
            dma((ITERS, n // group)),
        ],
        compiler_params=pltpu.CompilerParams(
            collective_id=0, has_side_effects=True, vmem_limit_bytes=56 * 1024 * 1024
        ),
    )(block_count, col_ids.T, send_ids.T, start, mixing, weights)
    return out


def solution(mesh):
    in_specs = (
        P("cols", "rows"),
        P("rows", None, None, None),
        P("rows"),
        P("rows", None),
        P("rows", None),
        P(),
    )
    out_specs = P("cols", "rows")
    return jax.shard_map(body, mesh=mesh, in_specs=in_specs, out_specs=out_specs, check_vma=False)
```
